32 devices in a mesh: dom: 8 (over z, y), sub: 4 (over x, core).
Axes of the slice: x: 2, y: 2, z: 4, core: 2. Of those that a mesh axis runs over, the one named last changes fastest.
Arguments:
- leaf_hist: float32 [112, 65536], P(None, ('dom', 'sub')), may hold values from -6 to 6
- leaf_weight: float32 [65536], P(('dom', 'sub')), may hold values from 0.1 to 1
- leaf_parent: int32 [65536], P(('dom', 'sub')), may hold values from 0 to 2047, as said below
- entry_parent: int32 [16384], P(('dom', 'sub')), may hold values from 0 to 511
- entry_dest: int32 [16384, 1], P(('dom', 'sub')), may hold values from 0 to 7; in each aligned block of 512 rows (0 to 511, 512 to 1023, ...) at most 256 rows name the same one
- entry_crash: int32 [16384], P(('dom', 'sub')), may hold values from 0 to 511
- entry_weight: float32 [16384], P(('dom', 'sub')), may hold values from 0.05 to 1
Outputs:
- crash_hist: float32 [80, 16384], P(None, ('dom', 'sub'))
The draws below stay inside these ranges and needn't reach their ends.
Inputs may be any that keep to these rules, and one draw needn't show every extreme that they name: `leaf_parent`: a leaf's parent is numbered 0 to 2047 within the leaves of its index of dom; every parent has at least one leaf. `entry_dest`: among the 512 entries of one device no index of dom is named more than 256 times.
All inputs are finite; a program needn't handle non-finite values.
Results may differ from the reference program's by a relative error of at most 0.00011.
Values sent between devices are 32-bit elements; how exact they have to be, the bound alone decides.
A program may use at most 64 MiB of HBM per device.

```python
import math
import jax
import jax.numpy as jnp
import numpy as np
from jax import lax

HIST = 16
THICK = 7
CTHICK = 5
LEAF_DEV = 2048
PAR_DEV = 512
ENT_DEV = 512
CRASH_DEV = 512
CAP = 256
LEAVES = 65536
PARENTS = 16384
ENTRIES = 16384
CRASH = 16384
N_DOM = 8
N_SUB = 4


def draw_leaf_parent(key, part):
    key = jax.random.fold_in(key, 11)
    group_leaves = LEAF_DEV * N_SUB
    group_parents = PAR_DEV * N_SUB
    extra_count = group_leaves - group_parents

    def one_group(group_key):
        key_reach, key_pick, key_shuffle = jax.random.split(group_key, 3)
        reach = jax.random.randint(key_reach, (extra_count,), 1, group_parents + 1, dtype=jnp.int32)
        extra = jax.random.randint(key_pick, (extra_count,), 0, reach, dtype=jnp.int32)
        base = jnp.concatenate([jnp.arange(group_parents, dtype=jnp.int32), extra])
        return jax.random.permutation(key_shuffle, base)
    group_keys = jax.random.split(key, N_DOM)
    return jax.vmap(one_group)(group_keys).reshape(-1).astype(jnp.int32)


def plant(array, stream_key, smallest, largest):
    longest = array.shape.index(max(array.shape))
    spots = []
    for shift in (0, 1):
        where = [jax.random.randint(jax.random.fold_in(stream_key, axis), (), 0, length) for axis, length in enumerate(array.shape)]
        where[longest] = (where[longest] + shift) % array.shape[longest]
        spots.append(tuple(where))
    return array.at[spots[0]].set(smallest).at[spots[1]].set(largest)


def level_of(stream_key, dims, cuts, smallest, top_value):
    def one(dim, shards_of):
        steps = jax.random.uniform(jax.random.fold_in(jax.random.fold_in(stream_key, 6), dim), (shards_of,), jnp.float32, smallest / len(cuts), top_value / len(cuts))
        return jnp.repeat(jnp.exp(steps), dims[dim] // shards_of).reshape((-1,) + (1,) * (len(dims) - dim - 1))

    gain = one(*cuts[0])
    for cut in cuts[1:]:
        gain = gain * one(*cut)
    return gain


def routed_block(key, own, number, rows, number_of, top, most, lean):
    ranking = jax.random.permutation(key, number_of)
    packed, ordinary = load_shares(number_of, rows * top, most, lean, True), load_shares(number_of, rows * top, most, lean, False)
    places = jnp.arange(number_of)

    def named(sizes, turn):
        used = int((sizes > 0).sum())
        fixed = max(1, used // 4)
        moved = fixed + (places - fixed + turn * (used - fixed)) % max(1, number_of - fixed)
        return jnp.zeros((number_of,), jnp.int32).at[ranking[jnp.where(places < fixed, places, moved)]].set(jnp.asarray(sizes, jnp.int32))

    sizes = jnp.where(number % 4 == 0, named(packed, number // 4), named(ordinary, number - number // 4 - 1))
    mixed = jax.random.permutation(jax.random.fold_in(own, 3), number_of)
    giver, sink = mixed[0:number_of // 2 * 2:2], mixed[1:number_of // 2 * 2:2]
    slack = jnp.minimum(sizes[giver] - 1, most - sizes[sink]) // 2
    slack = jnp.where((giver == ranking[0]) | (sink == ranking[0]) | (sizes[sink] == 0), 0, jnp.maximum(slack, 0))
    moved = jax.random.randint(jax.random.fold_in(own, 4), (number_of // 2,), 0, 1 << 20) % (slack + 1)
    sizes = sizes.at[giver].add(-moved).at[sink].add(moved)
    members = jnp.searchsorted(jnp.cumsum(sizes), jnp.arange(rows * top), side="right").astype(jnp.int32)
    table = members.reshape(top, rows).T
    table = table[jax.random.permutation(jax.random.fold_in(own, 1), rows)]
    turn = jax.random.randint(jax.random.fold_in(own, 2), (rows, 1), 0, top)
    return jnp.take_along_axis(table, (jnp.arange(top)[None, :] + turn) % top, axis=1)


def load_shares(count, total, bound, skew, full):
    portions = [(1 << 20) // math.isqrt(standing ** skew) + 1 for standing in range(1, count + 1)]
    largest = bound if full else min(bound, max(-(-total // count), total * portions[0] // sum(portions)))
    least = 1 if total - largest >= count - 1 else 0
    given, surplus = [largest] + [least] * (count - 1), total - largest - least * (count - 1)
    while surplus > 0:
        candidates = [i for i in range(1, count) if given[i] < largest] or [i for i in range(1, count) if given[i] < bound]
        mass, left = sum([portions[i] for i in candidates]), surplus
        for i in candidates:
            more = min(bound - given[i], max(1, left * portions[i] // mass), surplus)
            given[i] = given[i] + more
            surplus = surplus - more
    return np.array(given)


def bell_draw(stream_key, extent, deviation, limit, cuts=(), kind=jnp.bfloat16):
    factor_of = level_of(stream_key, extent, cuts, -0.22, 0.18) if cuts else 1.0
    values = jax.random.normal(stream_key, extent, jnp.float32) * deviation * factor_of
    return jnp.minimum(jnp.maximum(values, -limit), limit).astype(kind)


def setup_inputs(seed: int = 0) -> dict:
    streams_of = jax.random.split(jax.random.key(seed), 8)
    leaf_hist = bell_draw(streams_of[0], (HIST * THICK, LEAVES), 1.0, 6.0, ((1, 32),), jnp.float32)
    leaf_weight = jnp.clip(jnp.exp(math.log(1.0) - 2.3025851 * jax.random.uniform(streams_of[1], (LEAVES,), jnp.float32) ** level_of(streams_of[1], (LEAVES,), ((0, 32),), -0.2, 0.2)), 0.1, 1.0)
    leaf_parent = draw_leaf_parent(jax.random.fold_in(streams_of[7], 71), 0)
    entry_parent = plant(jax.random.randint(streams_of[3], (ENTRIES,), 0, PAR_DEV), jax.random.fold_in(streams_of[3], 1), 0, PAR_DEV - 1).astype(jnp.int32)
    entry_dest_keys = jax.random.split(jax.random.fold_in(streams_of[4], 1), ENTRIES // ENT_DEV)
    entry_dest_turns = jax.random.permutation(jax.random.fold_in(streams_of[4], 3), ENTRIES // ENT_DEV)
    entry_dest = jax.vmap(lambda own, number: routed_block(jax.random.fold_in(streams_of[4], 2), own, number, ENT_DEV, N_DOM, 1, CAP, 2))(entry_dest_keys, entry_dest_turns).reshape((ENTRIES, 1))
    entry_crash = plant(jax.random.randint(streams_of[5], (ENTRIES,), 0, CRASH_DEV), jax.random.fold_in(streams_of[5], 1), 0, CRASH_DEV - 1).astype(jnp.int32)
    entry_weight = jnp.clip(jnp.exp(math.log(1.0) - 2.9957323 * jax.random.uniform(streams_of[6], (ENTRIES,), jnp.float32) ** level_of(streams_of[6], (ENTRIES,), ((0, 32),), -0.2, 0.2)), 0.05, 1.0)
    return {"leaf_hist": leaf_hist, "leaf_weight": leaf_weight, "leaf_parent": leaf_parent, "entry_parent": entry_parent, "entry_dest": entry_dest, "entry_crash": entry_crash, "entry_weight": entry_weight}


def remap_table():
    target = jnp.arange(CTHICK, dtype=jnp.float32) * ((THICK - 1) / (CTHICK - 1))
    source = jnp.arange(THICK, dtype=jnp.float32)
    return jnp.maximum(0.0, 1.0 - jnp.abs(target[:, None] - source[None, :]))


def remap_rows(values):
    columns = values.shape[1]
    cube = values.reshape(HIST, THICK, columns)
    result = jnp.einsum("ct,htn->hcn", remap_table(), cube, precision=lax.Precision.HIGHEST)
    return result.reshape(HIST * CTHICK, columns)


def reference(leaf_hist, leaf_weight, leaf_parent, entry_parent, entry_dest, entry_crash, entry_weight):
    leaf_group = jnp.arange(LEAVES, dtype=jnp.int32) // (LEAF_DEV * N_SUB)
    parent_index = leaf_group * (PAR_DEV * N_SUB) + leaf_parent
    weighted = (leaf_hist * leaf_weight[None, :]).T
    parent_sums = jax.ops.segment_sum(weighted, parent_index, num_segments=PARENTS)
    parent_weight = jax.ops.segment_sum(leaf_weight, parent_index, num_segments=PARENTS)
    parent_hist = (parent_sums / parent_weight[:, None]).T
    remapped = remap_rows(parent_hist)
    device_index = jnp.arange(ENTRIES, dtype=jnp.int32) // ENT_DEV
    sub_index = device_index % N_SUB
    global_parent = device_index * PAR_DEV + entry_parent
    global_crash = (entry_dest[:, 0] * N_SUB + sub_index) * CRASH_DEV + entry_crash
    carried = jnp.take(remapped, global_parent, axis=1) * entry_weight[None, :]
    crash_sums = jax.ops.segment_sum(carried.T, global_crash, num_segments=CRASH)
    crash_weight = jax.ops.segment_sum(entry_weight, global_crash, num_segments=CRASH)
    return (crash_sums / jnp.maximum(crash_weight, 1.0)[:, None]).T
```

```python
import functools

import jax
import jax.numpy as jnp
from jax import lax
from jax.experimental import pallas as pl
from jax.experimental.pallas import tpu as pltpu
from jax.sharding import PartitionSpec as P

HIST = 16
THICK = 7
CTHICK = 5
PAR_DEV = 512
ENT_DEV = 512
CRASH_DEV = 512


def remap_table():
    target = jnp.arange(CTHICK, dtype=jnp.float32) * ((THICK - 1) / (CTHICK - 1))
    source = jnp.arange(THICK, dtype=jnp.float32)
    return jnp.maximum(0.0, 1.0 - jnp.abs(target[:, None] - source[None, :]))


def remap_rows(values):
    columns = values.shape[1]
    cube = values.reshape(HIST, THICK, columns)
    result = jnp.einsum("ct,htn->hcn", remap_table(), cube, precision=lax.Precision.HIGHEST)
    return result.reshape(HIST * CTHICK, columns)


def per_device(
    leaf_hist, leaf_weight, leaf_parent, entry_parent, entry_dest, entry_crash, entry_weight
):
    sub_total = lax.axis_size("sub")
    dom_total = lax.axis_size("dom")
    group_parents = PAR_DEV * sub_total
    weighted = (leaf_hist * leaf_weight[None, :]).T
    partial_sums = jax.ops.segment_sum(weighted, leaf_parent, num_segments=group_parents).T
    partial_weight = jax.ops.segment_sum(leaf_weight, leaf_parent, num_segments=group_parents)
    parent_sums, parent_weight = (
        lax.psum_scatter(partial_sums, "sub", scatter_dimension=1, tiled=True),
        lax.psum_scatter(partial_weight, "sub", scatter_dimension=0, tiled=True),
    )
    parent_hist = parent_sums / parent_weight[None, :]
    parent_hist = remap_rows(parent_hist)
    capacity = max(2, 4 * ENT_DEV // dom_total)
    slot_total = dom_total * capacity
    destination = entry_dest[:, 0]
    entry_total = destination.shape[0]
    ordering = jnp.argsort(destination, stable=True)
    sorted_destination = destination[ordering]
    first_slot = jnp.searchsorted(sorted_destination, sorted_destination, side="left")
    positions = jnp.arange(entry_total, dtype=jnp.int32)
    slot_sorted = sorted_destination * capacity + (positions - first_slot)
    slot_index = jnp.zeros((entry_total,), jnp.int32).at[ordering].set(slot_sorted)
    carried = jnp.take(parent_hist, entry_parent, axis=1) * entry_weight[None, :]
    send_values = (
        jnp.zeros((carried.shape[0], slot_total), jnp.float32).at[:, slot_index].set(carried)
    )
    send_weight = jnp.zeros((1, slot_total), jnp.float32).at[0, slot_index].set(entry_weight)
    send_crash = jnp.zeros((1, slot_total), jnp.int32).at[0, slot_index].set(entry_crash)
    got_values, got_weight, got_crash = (
        lax.all_to_all(send_values, "dom", split_axis=1, concat_axis=1, tiled=True),
        lax.all_to_all(send_weight, "dom", split_axis=1, concat_axis=1, tiled=True),
        lax.all_to_all(send_crash, "dom", split_axis=1, concat_axis=1, tiled=True),
    )
    crash_sums = jax.ops.segment_sum(got_values.T, got_crash[0], num_segments=CRASH_DEV).T
    crash_weight = jax.ops.segment_sum(got_weight[0], got_crash[0], num_segments=CRASH_DEV)
    return crash_sums / jnp.maximum(crash_weight, 1.0)[None, :]


MESH = pl.DeviceIdType.MESH
F32, BF16, I32 = jnp.float32, jnp.bfloat16, jnp.int32
HEAD = 8
ROWS = HIST * CTHICK
CHUNKS = 2


def dot_nn(a, b):
    return lax.dot_general(a, b, (((1,), (0,)), ((), ())), preferred_element_type=F32)


def dot_nt(a, b):
    return lax.dot_general(a, b, (((1,), (1,)), ((), ())), preferred_element_type=F32)


def terms(x, count):
    parts = []
    for _ in range(count):
        part = x.astype(BF16).astype(F32)
        parts.append(part)
        x = x - part
    return jnp.concatenate(parts, axis=0).astype(BF16)


def fold(x, count):
    rows = x.shape[0] // count
    total = x[:rows]
    for i in range(1, count):
        total = total + x[i * rows : (i + 1) * rows]
    return total


def one_hot(index_row, rows):
    step = min(rows, 256)
    count = index_row.shape[1]
    iota = lax.broadcasted_iota(I32, (step, count), 0).astype(F32).astype(BF16)
    one, zero = jnp.ones((), BF16), jnp.zeros((), BF16)
    blocks = []
    for base in range(0, rows, step):
        low = index_row - base
        low = jnp.where((low >= 0) & (low < step), low, -1).astype(F32).astype(BF16)
        blocks.append(jnp.where(iota == low, one, zero))
    return jnp.concatenate(blocks, axis=0) if len(blocks) > 1 else blocks[0]


def remap_matrix():
    row = lax.broadcasted_iota(I32, (ROWS, HIST * THICK), 0)
    column = lax.broadcasted_iota(I32, (ROWS, HIST * THICK), 1)
    row_h = (row * 205) >> 10
    column_h = (column * 147) >> 10
    target = (row - row_h * CTHICK).astype(F32) * ((THICK - 1) / (CTHICK - 1))
    source = (column - column_h * THICK).astype(F32)
    weight = jnp.maximum(0.0, 1.0 - jnp.abs(target - source))
    return jnp.where(row_h == column_h, weight, 0.0).astype(BF16)


def fused_kernel(
    n_dom, capacity,
    hist_hbm, leaf_weight, leaf_parent, entry_parent, entry_dest, entry_crash, entry_weight,
    out_ref,
    hist, data, kept, core_send, core_recv, x_send, x_recv, meta, meta_recv, pick, drop, pay, pay_recv, total,
    hist_sem, core_ssem, core_rsem, x_ssem, x_rsem, meta_ssem, meta_rsem, pay_ssem, pay_rsem,
):
    dom, sub = lax.axis_index("dom"), lax.axis_index("sub")
    load = pltpu.make_async_copy(hist_hbm, hist, hist_sem)
    load.start()
    core = lax.rem(sub, 2)
    x = sub // 2
    core_peer = (dom, x * 2 + 1 - core)
    x_peer = (dom, (1 - x) * 2 + core)

    def dom_of(mask):
        peer = jnp.zeros((), I32)
        bit = 1
        while bit < n_dom:
            own = lax.rem(dom // bit, 2)
            peer = peer + bit * (1 - own if mask & bit else own)
            bit *= 2
        return peer

    dom_peers = [(dom_of(mask), sub) for mask in range(n_dom)]
    barrier = pltpu.get_barrier_semaphore()
    for peer in [core_peer, x_peer] + dom_peers[1:]:
        pl.semaphore_signal(barrier, inc=1, device_id=peer, device_id_type=MESH)

    def remote(source, target, ssem, rsem, peer):
        return pltpu.make_async_remote_copy(
            src_ref=source, dst_ref=target, send_sem=ssem, recv_sem=rsem, device_id=peer, device_id_type=MESH
        )

    load.wait()
    high = hist[...].astype(BF16)
    low = (hist[...] - high.astype(F32)).astype(BF16)
    table = remap_matrix()
    remapped = dot_nn(table, high) + dot_nn(table, low)
    weight = leaf_weight[...]
    first = lax.broadcasted_iota(I32, (HEAD, weight.shape[1]), 0) == 0
    head = jnp.where(first, weight, 0.0)
    data[...] = terms(jnp.concatenate([head, remapped * weight], axis=0), 2)

    def quarter(index):
        return fold(dot_nt(data[...], one_hot(leaf_parent[...] - index * PAR_DEV, PAR_DEV)), 2)

    core_copies = [
        remote(core_send.at[i], core_recv.at[i], core_ssem.at[i], core_rsem.at[i], core_peer) for i in range(2)
    ]
    bounds = [0] + [HEAD + ROWS * (c + 1) // CHUNKS for c in range(CHUNKS)]
    spans = [pl.ds(bounds[c], bounds[c + 1] - bounds[c]) for c in range(CHUNKS)]
    x_copies = [
        remote(x_send.at[span], x_recv.at[span], x_ssem.at[c], x_rsem.at[c], x_peer) for c, span in enumerate(spans)
    ]
    core_send[0] = quarter((1 - x) * 2 + 1 - core)
    pl.semaphore_wait(barrier, n_dom + 1)
    core_copies[0].start()
    kept[0] = quarter((1 - x) * 2 + core)
    core_copies[0].wait_recv()
    for c, span in enumerate(spans):
        x_send[span] = kept[0, span] + core_recv[0, span]
        x_copies[c].start()
    core_send[1] = quarter(x * 2 + 1 - core)
    core_copies[1].start()
    kept[1] = quarter(x * 2 + core)

    entries = entry_parent.shape[1]
    named = entry_dest[...]
    mask = jnp.zeros_like(named)
    bit = 1
    while bit < n_dom:
        own = lax.rem(dom // bit, 2)
        part = lax.rem(named // bit, 2)
        mask = mask + bit * jnp.abs(part - own)
        bit *= 2
    padded = max(n_dom, 8)
    is_dest = (lax.broadcasted_iota(I32, (padded, entries), 0) == mask).astype(F32)
    earlier = lax.broadcasted_iota(I32, (entries, entries), 0) < lax.broadcasted_iota(I32, (entries, entries), 1)
    before = dot_nn(is_dest.astype(BF16), earlier.astype(F32).astype(BF16))
    rank = jnp.sum(before * is_dest, axis=0, keepdims=True).astype(I32)
    slot = mask * capacity + rank
    rows = jnp.concatenate(
        [
            entry_weight[...],
            entry_crash[...].astype(F32),
            entry_parent[...].astype(F32),
            jnp.zeros((5, entries), F32),
        ],
        axis=0,
    )
    rows = terms(rows, 3)
    for m in range(n_dom):
        meta[m] = fold(dot_nt(rows, one_hot(slot - m * capacity, capacity)), 3)
    meta_copies = {
        m: remote(meta.at[m], meta_recv.at[m], meta_ssem.at[m], meta_rsem.at[m], dom_peers[m])
        for m in range(1, n_dom)
    }
    for copy in meta_copies.values():
        copy.start()
    for m in range(n_dom):
        pick[m] = one_hot(meta[m, 2:3].astype(I32), PAR_DEV)

    core_copies[1].wait_recv()
    pay_copies = {}
    inverse = None
    for c, span in enumerate(spans):
        x_copies[c].wait_recv()
        sums = kept[1, span] + core_recv[1, span] + x_recv[span]
        if c == 0:
            inverse = 1.0 / sums[:1]
            sums = sums[HEAD:]
        means = terms(sums * inverse, 2)
        for m in list(range(n_dom - 1, -1, -1)):
            pay[c, m] = fold(dot_nn(means, pick[m]), 2) * meta[m, :1]
            if m:
                copy = remote(pay.at[c, m], pay_recv.at[c, m], pay_ssem.at[c, m], pay_rsem.at[c, m], dom_peers[m])
                copy.start()
                pay_copies[c, m] = copy

    crash_weight = jnp.zeros((1, CRASH_DEV), F32)
    for m in range(n_dom):
        if m:
            meta_copies[m].wait_recv()
        got = meta_recv[m] if m else meta[0]
        drop[m] = one_hot(got[1:2].astype(I32), CRASH_DEV)
        crash_weight = crash_weight + fold(dot_nt(terms(got, 3), drop[m]), 3)[:1]
    inverse = 1.0 / jnp.maximum(crash_weight, 1.0)
    size = ROWS // CHUNKS
    for c in range(CHUNKS):
        total[...] = dot_nt(terms(pay[c, 0], 2), drop[0])
        for m in list(range(n_dom - 1, 0, -1)):
            pay_copies[c, m].wait_recv()
            total[...] += dot_nt(terms(pay_recv[c, m], 2), drop[m])
        out_ref[pl.ds(c * size, size)] = fold(total[...], 2) * inverse
    for copy in core_copies + x_copies + list(meta_copies.values()) + list(pay_copies.values()):
        copy.wait_send()


def fused(leaf_hist, leaf_weight, leaf_parent, entry_parent, entry_dest, entry_crash, entry_weight):
    n_dom = lax.axis_size("dom")
    capacity = 4 * ENT_DEV // n_dom
    leaves = leaf_hist.shape[1]
    size = ROWS // CHUNKS
    vmem = pl.BlockSpec(memory_space=pltpu.VMEM)
    dma = pltpu.SemaphoreType.DMA
    row = lambda array: array.reshape(1, -1)
    return pl.pallas_call(
        functools.partial(fused_kernel, n_dom, capacity),
        out_shape=jax.ShapeDtypeStruct((ROWS, CRASH_DEV), F32),
        in_specs=[pl.BlockSpec(memory_space=pl.ANY)] + [vmem] * 6,
        out_specs=vmem,
        scratch_shapes=[
            pltpu.VMEM((HIST * THICK, leaves), F32),
            pltpu.VMEM((2 * (HEAD + ROWS), leaves), BF16),
            pltpu.VMEM((2, HEAD + ROWS, PAR_DEV), F32),
            pltpu.VMEM((2, HEAD + ROWS, PAR_DEV), F32),
            pltpu.VMEM((2, HEAD + ROWS, PAR_DEV), F32),
            pltpu.VMEM((HEAD + ROWS, PAR_DEV), F32),
            pltpu.VMEM((HEAD + ROWS, PAR_DEV), F32),
            pltpu.VMEM((n_dom, 8, capacity), F32),
            pltpu.VMEM((n_dom, 8, capacity), F32),
            pltpu.VMEM((n_dom, PAR_DEV, capacity), BF16),
            pltpu.VMEM((n_dom, CRASH_DEV, capacity), BF16),
            pltpu.VMEM((CHUNKS, n_dom, size, capacity), F32),
            pltpu.VMEM((CHUNKS, n_dom, size, capacity), F32),
            pltpu.VMEM((2 * size, CRASH_DEV), F32),
            dma,
            dma((2,)),
            dma((2,)),
            dma((CHUNKS,)),
            dma((CHUNKS,)),
            dma((n_dom,)),
            dma((n_dom,)),
            dma((CHUNKS, n_dom)),
            dma((CHUNKS, n_dom)),
        ],
        compiler_params=pltpu.CompilerParams(
            collective_id=0, has_side_effects=True, vmem_limit_bytes=48 * 1024 * 1024
        ),
    )(
        leaf_hist, row(leaf_weight), row(leaf_parent), row(entry_parent), row(entry_dest), row(entry_crash),
        row(entry_weight),
    )


def solution(mesh):
    n_dom, n_sub = mesh.shape["dom"], mesh.shape["sub"]
    aligned = n_dom & (n_dom - 1) == 0 and n_dom <= 8 and (4 * ENT_DEV // n_dom) % 128 == 0 and n_sub == 4
    in_specs = (
        P(None, ("dom", "sub")),
        P(("dom", "sub")),
        P(("dom", "sub")),
        P(("dom", "sub")),
        P(("dom", "sub"), None),
        P(("dom", "sub")),
        P(("dom", "sub")),
    )
    out_specs = P(None, ("dom", "sub"))
    return jax.shard_map(
        fused if aligned else per_device, mesh=mesh, in_specs=in_specs, out_specs=out_specs, check_vma=False
    )
```

```python
import functools

import jax
import jax.numpy as jnp
from jax import lax
from jax.experimental import pallas as pl
from jax.experimental.pallas import tpu as pltpu
from jax.sharding import PartitionSpec as P

HIST = 16
THICK = 7
CTHICK = 5
PAR_DEV = 512
ENT_DEV = 512
CRASH_DEV = 512


def remap_table():
    target = jnp.arange(CTHICK, dtype=jnp.float32) * ((THICK - 1) / (CTHICK - 1))
    source = jnp.arange(THICK, dtype=jnp.float32)
    return jnp.maximum(0.0, 1.0 - jnp.abs(target[:, None] - source[None, :]))


def remap_rows(values):
    columns = values.shape[1]
    cube = values.reshape(HIST, THICK, columns)
    result = jnp.einsum("ct,htn->hcn", remap_table(), cube, precision=lax.Precision.HIGHEST)
    return result.reshape(HIST * CTHICK, columns)


def per_device(
    leaf_hist, leaf_weight, leaf_parent, entry_parent, entry_dest, entry_crash, entry_weight
):
    sub_total = lax.axis_size("sub")
    dom_total = lax.axis_size("dom")
    group_parents = PAR_DEV * sub_total
    weighted = (leaf_hist * leaf_weight[None, :]).T
    partial_sums = jax.ops.segment_sum(weighted, leaf_parent, num_segments=group_parents).T
    partial_weight = jax.ops.segment_sum(leaf_weight, leaf_parent, num_segments=group_parents)
    parent_sums, parent_weight = (
        lax.psum_scatter(partial_sums, "sub", scatter_dimension=1, tiled=True),
        lax.psum_scatter(partial_weight, "sub", scatter_dimension=0, tiled=True),
    )
    parent_hist = parent_sums / parent_weight[None, :]
    parent_hist = remap_rows(parent_hist)
    capacity = max(2, 4 * ENT_DEV // dom_total)
    slot_total = dom_total * capacity
    destination = entry_dest[:, 0]
    entry_total = destination.shape[0]
    ordering = jnp.argsort(destination, stable=True)
    sorted_destination = destination[ordering]
    first_slot = jnp.searchsorted(sorted_destination, sorted_destination, side="left")
    positions = jnp.arange(entry_total, dtype=jnp.int32)
    slot_sorted = sorted_destination * capacity + (positions - first_slot)
    slot_index = jnp.zeros((entry_total,), jnp.int32).at[ordering].set(slot_sorted)
    carried = jnp.take(parent_hist, entry_parent, axis=1) * entry_weight[None, :]
    send_values = (
        jnp.zeros((carried.shape[0], slot_total), jnp.float32).at[:, slot_index].set(carried)
    )
    send_weight = jnp.zeros((1, slot_total), jnp.float32).at[0, slot_index].set(entry_weight)
    send_crash = jnp.zeros((1, slot_total), jnp.int32).at[0, slot_index].set(entry_crash)
    got_values, got_weight, got_crash = (
        lax.all_to_all(send_values, "dom", split_axis=1, concat_axis=1, tiled=True),
        lax.all_to_all(send_weight, "dom", split_axis=1, concat_axis=1, tiled=True),
        lax.all_to_all(send_crash, "dom", split_axis=1, concat_axis=1, tiled=True),
    )
    crash_sums = jax.ops.segment_sum(got_values.T, got_crash[0], num_segments=CRASH_DEV).T
    crash_weight = jax.ops.segment_sum(got_weight[0], got_crash[0], num_segments=CRASH_DEV)
    return crash_sums / jnp.maximum(crash_weight, 1.0)[None, :]


MESH = pl.DeviceIdType.MESH
F32, BF16, I32 = jnp.float32, jnp.bfloat16, jnp.int32
HEAD = 8
ROWS = HIST * CTHICK
CHUNKS = 2


def dot_nn(a, b):
    return lax.dot_general(a, b, (((1,), (0,)), ((), ())), preferred_element_type=F32)


def dot_nt(a, b):
    return lax.dot_general(a, b, (((1,), (1,)), ((), ())), preferred_element_type=F32)


def terms(x, count):
    parts = []
    for _ in range(count):
        part = x.astype(BF16).astype(F32)
        parts.append(part)
        x = x - part
    return jnp.concatenate(parts, axis=0).astype(BF16)


def fold(x, count):
    rows = x.shape[0] // count
    total = x[:rows]
    for i in range(1, count):
        total = total + x[i * rows : (i + 1) * rows]
    return total


def one_hot(index_row, rows):
    step = min(rows, 256)
    count = index_row.shape[1]
    iota = lax.broadcasted_iota(I32, (step, count), 0).astype(F32).astype(BF16)
    one, zero = jnp.ones((), BF16), jnp.zeros((), BF16)
    blocks = []
    for base in range(0, rows, step):
        low = index_row - base
        low = jnp.where((low >= 0) & (low < step), low, -1).astype(F32).astype(BF16)
        blocks.append(jnp.where(iota == low, one, zero))
    return jnp.concatenate(blocks, axis=0) if len(blocks) > 1 else blocks[0]


def remap_matrix():
    row = lax.broadcasted_iota(I32, (ROWS, HIST * THICK), 0)
    column = lax.broadcasted_iota(I32, (ROWS, HIST * THICK), 1)
    row_h = (row * 205) >> 10
    column_h = (column * 147) >> 10
    target = (row - row_h * CTHICK).astype(F32) * ((THICK - 1) / (CTHICK - 1))
    source = (column - column_h * THICK).astype(F32)
    weight = jnp.maximum(0.0, 1.0 - jnp.abs(target - source))
    return jnp.where(row_h == column_h, weight, 0.0).astype(BF16)


def fused_kernel(
    n_dom, capacity,
    hist_hbm, leaf_weight_hbm, leaf_parent_hbm, entry_parent_hbm, entry_dest_hbm, entry_crash_hbm, entry_weight_hbm,
    out_ref,
    hist, leaf_weight, leaf_parent, entry_parent, entry_dest, entry_crash, entry_weight, data, kept, core_send, core_recv, x_send, x_recv, meta, meta_recv, pick, drop, pay, pay_recv, total,
    load_sem, core_ssem, core_rsem, x_ssem, x_rsem, meta_ssem, meta_rsem, pay_ssem, pay_rsem,
):
    dom, sub = lax.axis_index("dom"), lax.axis_index("sub")
    pairs = [
        (leaf_parent_hbm, leaf_parent),
        (hist_hbm, hist),
        (leaf_weight_hbm, leaf_weight),
        (entry_dest_hbm, entry_dest),
        (entry_weight_hbm, entry_weight),
        (entry_crash_hbm, entry_crash),
        (entry_parent_hbm, entry_parent),
    ]
    loads = [pltpu.make_async_copy(source, target, load_sem.at[i]) for i, (source, target) in enumerate(pairs)]
    for load in loads:
        load.start()
    core = lax.rem(sub, 2)
    x = sub // 2
    core_peer = (dom, x * 2 + 1 - core)
    x_peer = (dom, (1 - x) * 2 + core)

    def dom_of(mask):
        peer = jnp.zeros((), I32)
        bit = 1
        while bit < n_dom:
            own = lax.rem(dom // bit, 2)
            peer = peer + bit * (1 - own if mask & bit else own)
            bit *= 2
        return peer

    dom_peers = [(dom_of(mask), sub) for mask in range(n_dom)]
    barrier = pltpu.get_barrier_semaphore()
    for peer in [core_peer, x_peer] + dom_peers[1:]:
        pl.semaphore_signal(barrier, inc=1, device_id=peer, device_id_type=MESH)

    def remote(source, target, ssem, rsem, peer):
        return pltpu.make_async_remote_copy(
            src_ref=source, dst_ref=target, send_sem=ssem, recv_sem=rsem, device_id=peer, device_id_type=MESH
        )

    loads[0].wait()
    first_hot = one_hot(leaf_parent[...] - ((1 - x) * 2 + 1 - core) * PAR_DEV, PAR_DEV)
    loads[1].wait()
    loads[2].wait()
    high = hist[...].astype(BF16)
    low = (hist[...] - high.astype(F32)).astype(BF16)
    table = remap_matrix()
    remapped = dot_nn(table, high) + dot_nn(table, low)
    weight = leaf_weight[...]
    first = lax.broadcasted_iota(I32, (HEAD, weight.shape[1]), 0) == 0
    head = jnp.where(first, weight, 0.0)
    data[...] = terms(jnp.concatenate([head, remapped * weight], axis=0), 2)

    def quarter(index):
        return fold(dot_nt(data[...], one_hot(leaf_parent[...] - index * PAR_DEV, PAR_DEV)), 2)

    core_copies = [
        remote(core_send.at[i], core_recv.at[i], core_ssem.at[i], core_rsem.at[i], core_peer) for i in range(2)
    ]
    bounds = [0] + [HEAD + ROWS * (c + 1) // CHUNKS for c in range(CHUNKS)]
    spans = [pl.ds(bounds[c], bounds[c + 1] - bounds[c]) for c in range(CHUNKS)]
    x_copies = [
        remote(x_send.at[span], x_recv.at[span], x_ssem.at[c], x_rsem.at[c], x_peer) for c, span in enumerate(spans)
    ]
    core_send[0] = fold(dot_nt(data[...], first_hot), 2)
    pl.semaphore_wait(barrier, n_dom + 1)
    core_copies[0].start()
    kept[0] = quarter((1 - x) * 2 + core)
    core_copies[0].wait_recv()
    for c, span in enumerate(spans):
        x_send[span] = kept[0, span] + core_recv[0, span]
        x_copies[c].start()
    core_send[1] = quarter(x * 2 + 1 - core)
    core_copies[1].start()
    kept[1] = quarter(x * 2 + core)

    for load in loads[3:]:
        load.wait()
    entries = entry_parent.shape[1]
    named = entry_dest[...]
    mask = jnp.zeros_like(named)
    bit = 1
    while bit < n_dom:
        own = lax.rem(dom // bit, 2)
        part = lax.rem(named // bit, 2)
        mask = mask + bit * jnp.abs(part - own)
        bit *= 2
    padded = max(n_dom, 8)
    is_dest = (lax.broadcasted_iota(I32, (padded, entries), 0) == mask).astype(F32)
    earlier = lax.broadcasted_iota(I32, (entries, entries), 0) < lax.broadcasted_iota(I32, (entries, entries), 1)
    before = dot_nn(is_dest.astype(BF16), earlier.astype(F32).astype(BF16))
    rank = jnp.sum(before * is_dest, axis=0, keepdims=True).astype(I32)
    slot = mask * capacity + rank
    rows = jnp.concatenate(
        [
            entry_weight[...],
            entry_crash[...].astype(F32),
            entry_parent[...].astype(F32),
            jnp.zeros((5, entries), F32),
        ],
        axis=0,
    )
    rows = terms(rows, 3)
    for m in range(n_dom):
        meta[m] = fold(dot_nt(rows, one_hot(slot - m * capacity, capacity)), 3)
    meta_copies = {
        m: remote(meta.at[m], meta_recv.at[m], meta_ssem.at[m], meta_rsem.at[m], dom_peers[m])
        for m in range(1, n_dom)
    }
    for copy in meta_copies.values():
        copy.start()
    for m in range(n_dom):
        pick[m] = one_hot(meta[m, 2:3].astype(I32), PAR_DEV)

    core_copies[1].wait_recv()
    pay_copies = {}
    inverse = None
    for c, span in enumerate(spans):
        x_copies[c].wait_recv()
        sums = kept[1, span] + core_recv[1, span] + x_recv[span]
        if c == 0:
            inverse = 1.0 / sums[:1]
            sums = sums[HEAD:]
        means = terms(sums * inverse, 2)
        for m in list(range(n_dom - 1, -1, -1)):
            pay[c, m] = fold(dot_nn(means, pick[m]), 2) * meta[m, :1]
            if m:
                copy = remote(pay.at[c, m], pay_recv.at[c, m], pay_ssem.at[c, m], pay_rsem.at[c, m], dom_peers[m])
                copy.start()
                pay_copies[c, m] = copy

    crash_weight = jnp.zeros((1, CRASH_DEV), F32)
    for m in range(n_dom):
        if m:
            meta_copies[m].wait_recv()
        got = meta_recv[m] if m else meta[0]
        drop[m] = one_hot(got[1:2].astype(I32), CRASH_DEV)
        crash_weight = crash_weight + fold(dot_nt(terms(got, 3), drop[m]), 3)[:1]
    inverse = 1.0 / jnp.maximum(crash_weight, 1.0)
    size = ROWS // CHUNKS
    for c in range(CHUNKS):
        total[...] = dot_nt(terms(pay[c, 0], 2), drop[0])
        for m in list(range(n_dom - 1, 0, -1)):
            pay_copies[c, m].wait_recv()
            total[...] += dot_nt(terms(pay_recv[c, m], 2), drop[m])
        out_ref[pl.ds(c * size, size)] = fold(total[...], 2) * inverse
    for copy in core_copies + x_copies + list(meta_copies.values()) + list(pay_copies.values()):
        copy.wait_send()


def fused(leaf_hist, leaf_weight, leaf_parent, entry_parent, entry_dest, entry_crash, entry_weight):
    n_dom = lax.axis_size("dom")
    capacity = 4 * ENT_DEV // n_dom
    leaves = leaf_hist.shape[1]
    size = ROWS // CHUNKS
    vmem = pl.BlockSpec(memory_space=pltpu.VMEM)
    dma = pltpu.SemaphoreType.DMA
    row = lambda array: array.reshape(1, -1)
    return pl.pallas_call(
        functools.partial(fused_kernel, n_dom, capacity),
        out_shape=jax.ShapeDtypeStruct((ROWS, CRASH_DEV), F32),
        in_specs=[pl.BlockSpec(memory_space=pltpu.HBM)] * 7,
        out_specs=vmem,
        scratch_shapes=[
            pltpu.VMEM((HIST * THICK, leaves), F32),
            pltpu.VMEM((1, leaves), F32),
            pltpu.VMEM((1, leaves), I32),
            pltpu.VMEM((1, ENT_DEV), I32),
            pltpu.VMEM((1, ENT_DEV), I32),
            pltpu.VMEM((1, ENT_DEV), I32),
            pltpu.VMEM((1, ENT_DEV), F32),
            pltpu.VMEM((2 * (HEAD + ROWS), leaves), BF16),
            pltpu.VMEM((2, HEAD + ROWS, PAR_DEV), F32),
            pltpu.VMEM((2, HEAD + ROWS, PAR_DEV), F32),
            pltpu.VMEM((2, HEAD + ROWS, PAR_DEV), F32),
            pltpu.VMEM((HEAD + ROWS, PAR_DEV), F32),
            pltpu.VMEM((HEAD + ROWS, PAR_DEV), F32),
            pltpu.VMEM((n_dom, 8, capacity), F32),
            pltpu.VMEM((n_dom, 8, capacity), F32),
            pltpu.VMEM((n_dom, PAR_DEV, capacity), BF16),
            pltpu.VMEM((n_dom, CRASH_DEV, capacity), BF16),
            pltpu.VMEM((CHUNKS, n_dom, size, capacity), F32),
            pltpu.VMEM((CHUNKS, n_dom, size, capacity), F32),
            pltpu.VMEM((2 * size, CRASH_DEV), F32),
            dma((7,)),
            dma((2,)),
            dma((2,)),
            dma((CHUNKS,)),
            dma((CHUNKS,)),
            dma((n_dom,)),
            dma((n_dom,)),
            dma((CHUNKS, n_dom)),
            dma((CHUNKS, n_dom)),
        ],
        compiler_params=pltpu.CompilerParams(
            collective_id=0, has_side_effects=True, vmem_limit_bytes=60 * 1024 * 1024
        ),
    )(
        leaf_hist, row(leaf_weight), row(leaf_parent), row(entry_parent), row(entry_dest), row(entry_crash),
        row(entry_weight),
    )


def solution(mesh):
    n_dom, n_sub = mesh.shape["dom"], mesh.shape["sub"]
    aligned = n_dom & (n_dom - 1) == 0 and n_dom <= 8 and (4 * ENT_DEV // n_dom) % 128 == 0 and n_sub == 4
    in_specs = (
        P(None, ("dom", "sub")),
        P(("dom", "sub")),
        P(("dom", "sub")),
        P(("dom", "sub")),
        P(("dom", "sub"), None),
        P(("dom", "sub")),
        P(("dom", "sub")),
    )
    out_specs = P(None, ("dom", "sub"))
    return jax.shard_map(
        fused if aligned else per_device, mesh=mesh, in_specs=in_specs, out_specs=out_specs, check_vma=False
    )
```

```python
import functools

import jax
import jax.numpy as jnp
from jax import lax
from jax.experimental import pallas as pl
from jax.experimental.pallas import tpu as pltpu
from jax.sharding import PartitionSpec as P

HIST = 16
THICK = 7
CTHICK = 5
PAR_DEV = 512
ENT_DEV = 512
CRASH_DEV = 512


def remap_table():
    target = jnp.arange(CTHICK, dtype=jnp.float32) * ((THICK - 1) / (CTHICK - 1))
    source = jnp.arange(THICK, dtype=jnp.float32)
    return jnp.maximum(0.0, 1.0 - jnp.abs(target[:, None] - source[None, :]))


def remap_rows(values):
    columns = values.shape[1]
    cube = values.reshape(HIST, THICK, columns)
    result = jnp.einsum("ct,htn->hcn", remap_table(), cube, precision=lax.Precision.HIGHEST)
    return result.reshape(HIST * CTHICK, columns)


def per_device(
    leaf_hist, leaf_weight, leaf_parent, entry_parent, entry_dest, entry_crash, entry_weight
):
    sub_total = lax.axis_size("sub")
    dom_total = lax.axis_size("dom")
    group_parents = PAR_DEV * sub_total
    weighted = (leaf_hist * leaf_weight[None, :]).T
    partial_sums = jax.ops.segment_sum(weighted, leaf_parent, num_segments=group_parents).T
    partial_weight = jax.ops.segment_sum(leaf_weight, leaf_parent, num_segments=group_parents)
    parent_sums, parent_weight = (
        lax.psum_scatter(partial_sums, "sub", scatter_dimension=1, tiled=True),
        lax.psum_scatter(partial_weight, "sub", scatter_dimension=0, tiled=True),
    )
    parent_hist = parent_sums / parent_weight[None, :]
    parent_hist = remap_rows(parent_hist)
    capacity = max(2, 4 * ENT_DEV // dom_total)
    slot_total = dom_total * capacity
    destination = entry_dest[:, 0]
    entry_total = destination.shape[0]
    ordering = jnp.argsort(destination, stable=True)
    sorted_destination = destination[ordering]
    first_slot = jnp.searchsorted(sorted_destination, sorted_destination, side="left")
    positions = jnp.arange(entry_total, dtype=jnp.int32)
    slot_sorted = sorted_destination * capacity + (positions - first_slot)
    slot_index = jnp.zeros((entry_total,), jnp.int32).at[ordering].set(slot_sorted)
    carried = jnp.take(parent_hist, entry_parent, axis=1) * entry_weight[None, :]
    send_values = (
        jnp.zeros((carried.shape[0], slot_total), jnp.float32).at[:, slot_index].set(carried)
    )
    send_weight = jnp.zeros((1, slot_total), jnp.float32).at[0, slot_index].set(entry_weight)
    send_crash = jnp.zeros((1, slot_total), jnp.int32).at[0, slot_index].set(entry_crash)
    got_values, got_weight, got_crash = (
        lax.all_to_all(send_values, "dom", split_axis=1, concat_axis=1, tiled=True),
        lax.all_to_all(send_weight, "dom", split_axis=1, concat_axis=1, tiled=True),
        lax.all_to_all(send_crash, "dom", split_axis=1, concat_axis=1, tiled=True),
    )
    crash_sums = jax.ops.segment_sum(got_values.T, got_crash[0], num_segments=CRASH_DEV).T
    crash_weight = jax.ops.segment_sum(got_weight[0], got_crash[0], num_segments=CRASH_DEV)
    return crash_sums / jnp.maximum(crash_weight, 1.0)[None, :]


MESH = pl.DeviceIdType.MESH
F32, BF16, I32 = jnp.float32, jnp.bfloat16, jnp.int32
HEAD = 8
ROWS = HIST * CTHICK
CHUNKS = 2


def dot_nn(a, b):
    return lax.dot_general(a, b, (((1,), (0,)), ((), ())), preferred_element_type=F32)


def dot_nt(a, b):
    return lax.dot_general(a, b, (((1,), (1,)), ((), ())), preferred_element_type=F32)


def terms(x, count):
    parts = []
    for _ in range(count):
        part = x.astype(BF16).astype(F32)
        parts.append(part)
        x = x - part
    return jnp.concatenate(parts, axis=0).astype(BF16)


def fold(x, count):
    rows = x.shape[0] // count
    total = x[:rows]
    for i in range(1, count):
        total = total + x[i * rows : (i + 1) * rows]
    return total


def one_hot(index_row, rows):
    step = min(rows, 256)
    count = index_row.shape[1]
    iota = lax.broadcasted_iota(I32, (step, count), 0).astype(F32).astype(BF16)
    one, zero = jnp.ones((), BF16), jnp.zeros((), BF16)
    blocks = []
    for base in range(0, rows, step):
        low = index_row - base
        low = jnp.where((low >= 0) & (low < step), low, -1).astype(F32).astype(BF16)
        blocks.append(jnp.where(iota == low, one, zero))
    return jnp.concatenate(blocks, axis=0) if len(blocks) > 1 else blocks[0]


def remap_matrix():
    row = lax.broadcasted_iota(I32, (ROWS, HIST * THICK), 0)
    column = lax.broadcasted_iota(I32, (ROWS, HIST * THICK), 1)
    row_h = (row * 205) >> 10
    column_h = (column * 147) >> 10
    target = (row - row_h * CTHICK).astype(F32) * ((THICK - 1) / (CTHICK - 1))
    source = (column - column_h * THICK).astype(F32)
    weight = jnp.maximum(0.0, 1.0 - jnp.abs(target - source))
    return jnp.where(row_h == column_h, weight, 0.0).astype(BF16)


def fused_kernel(
    n_dom, capacity,
    hist_hbm, leaf_weight_hbm, leaf_parent_hbm, entry_parent_hbm, entry_dest_hbm, entry_crash_hbm, entry_weight_hbm,
    out_ref,
    hist, leaf_weight, leaf_parent, entry_parent, entry_dest, entry_crash, entry_weight, data, kept, core_send, core_recv, x_send, x_recv, meta, meta_recv, pick, drop, pay, pay_recv, total,
    load_sem, core_ssem, core_rsem, x_ssem, x_rsem, meta_ssem, meta_rsem, pay_ssem, pay_rsem,
):
    dom, sub = lax.axis_index("dom"), lax.axis_index("sub")
    pairs = [
        (leaf_parent_hbm, leaf_parent),
        (hist_hbm, hist),
        (leaf_weight_hbm, leaf_weight),
        (entry_dest_hbm, entry_dest),
        (entry_weight_hbm, entry_weight),
        (entry_crash_hbm, entry_crash),
        (entry_parent_hbm, entry_parent),
    ]
    loads = [pltpu.make_async_copy(source, target, load_sem.at[i]) for i, (source, target) in enumerate(pairs)]
    for load in loads:
        load.start()
    core = lax.rem(sub, 2)
    x = sub // 2
    core_peer = (dom, x * 2 + 1 - core)
    x_peer = (dom, (1 - x) * 2 + core)

    def dom_of(mask):
        peer = jnp.zeros((), I32)
        bit = 1
        while bit < n_dom:
            own = lax.rem(dom // bit, 2)
            peer = peer + bit * (1 - own if mask & bit else own)
            bit *= 2
        return peer

    dom_peers = [(dom_of(mask), sub) for mask in range(n_dom)]
    barrier = pltpu.get_barrier_semaphore()
    for peer in [core_peer, x_peer] + dom_peers[1:]:
        pl.semaphore_signal(barrier, inc=1, device_id=peer, device_id_type=MESH)

    def remote(source, target, ssem, rsem, peer):
        return pltpu.make_async_remote_copy(
            src_ref=source, dst_ref=target, send_sem=ssem, recv_sem=rsem, device_id=peer, device_id_type=MESH
        )

    loads[0].wait()
    first_hot = one_hot(leaf_parent[...] - ((1 - x) * 2 + 1 - core) * PAR_DEV, PAR_DEV)
    loads[1].wait()
    loads[2].wait()
    high = hist[...].astype(BF16)
    low = (hist[...] - high.astype(F32)).astype(BF16)
    table = remap_matrix()
    remapped = dot_nn(table, high) + dot_nn(table, low)
    weight = leaf_weight[...]
    first = lax.broadcasted_iota(I32, (HEAD, weight.shape[1]), 0) == 0
    head = jnp.where(first, weight, 0.0)
    data[...] = terms(jnp.concatenate([head, remapped * weight], axis=0), 2)

    def quarter(index):
        return fold(dot_nt(data[...], one_hot(leaf_parent[...] - index * PAR_DEV, PAR_DEV)), 2)

    core_copies = [
        remote(core_send.at[i], core_recv.at[i], core_ssem.at[i], core_rsem.at[i], core_peer) for i in range(2)
    ]
    bounds = [0] + [HEAD + ROWS * (c + 1) // CHUNKS for c in range(CHUNKS)]
    spans = [pl.ds(bounds[c], bounds[c + 1] - bounds[c]) for c in range(CHUNKS)]
    x_copies = [
        remote(x_send.at[span], x_recv.at[span], x_ssem.at[c], x_rsem.at[c], x_peer) for c, span in enumerate(spans)
    ]
    core_send[0] = fold(dot_nt(data[...], first_hot), 2)
    pl.semaphore_wait(barrier, n_dom + 1)
    core_copies[0].start()
    kept[0] = quarter((1 - x) * 2 + core)
    core_copies[0].wait_recv()
    for c, span in enumerate(spans):
        x_send[span] = kept[0, span] + core_recv[0, span]
        x_copies[c].start()
    core_send[1] = quarter(x * 2 + 1 - core)
    core_copies[1].start()
    kept[1] = quarter(x * 2 + core)

    for load in loads[3:]:
        load.wait()
    entries = entry_parent.shape[1]
    named = entry_dest[...]
    mask = jnp.zeros_like(named)
    bit = 1
    while bit < n_dom:
        own = lax.rem(dom // bit, 2)
        part = lax.rem(named // bit, 2)
        mask = mask + bit * jnp.abs(part - own)
        bit *= 2
    padded = max(n_dom, 8)
    is_dest = (lax.broadcasted_iota(I32, (padded, entries), 0) == mask).astype(F32)
    earlier = lax.broadcasted_iota(I32, (entries, entries), 0) < lax.broadcasted_iota(I32, (entries, entries), 1)
    before = dot_nn(is_dest.astype(BF16), earlier.astype(F32).astype(BF16))
    rank = jnp.sum(before * is_dest, axis=0, keepdims=True).astype(I32)
    slot = mask * capacity + rank
    rows = jnp.concatenate(
        [
            entry_weight[...],
            entry_crash[...].astype(F32),
            entry_parent[...].astype(F32),
            jnp.zeros((5, entries), F32),
        ],
        axis=0,
    )
    rows = terms(rows, 3)
    for m in range(n_dom):
        meta[m] = fold(dot_nt(rows, one_hot(slot - m * capacity, capacity)), 3)
    meta_copies = {
        m: remote(meta.at[m], meta_recv.at[m], meta_ssem.at[m], meta_rsem.at[m], dom_peers[m])
        for m in range(1, n_dom)
    }
    for copy in meta_copies.values():
        copy.start()
    for m in range(n_dom):
        pick[m] = one_hot(meta[m, 2:3].astype(I32), PAR_DEV)

    core_copies[1].wait_recv()
    pay_copies = {}
    inverse = None
    for c, span in enumerate(spans):
        x_copies[c].wait_recv()
        sums = kept[1, span] + core_recv[1, span] + x_recv[span]
        if c == 0:
            inverse = 1.0 / sums[:1]
            sums = sums[HEAD:]
        means = terms(sums * inverse, 2)
        for m in list(range(n_dom - 1, -1, -1)):
            pay[c, m] = fold(dot_nn(means, pick[m]), 2) * meta[m, :1]
            if m:
                copy = remote(pay.at[c, m], pay_recv.at[c, m], pay_ssem.at[c, m], pay_rsem.at[c, m], dom_peers[m])
                copy.start()
                pay_copies[c, m] = copy

    crash_weight = jnp.zeros((1, CRASH_DEV), F32)
    for m in range(n_dom):
        if m:
            meta_copies[m].wait_recv()
        got = meta_recv[m] if m else meta[0]
        drop[m] = one_hot(got[1:2].astype(I32), CRASH_DEV)
        crash_weight = crash_weight + fold(dot_nt(terms(got, 3), drop[m]), 3)[:1]
    inverse = 1.0 / jnp.maximum(crash_weight, 1.0)
    size = ROWS // CHUNKS
    for c in range(CHUNKS):
        total[...] = dot_nt(terms(pay[c, 0], 2), drop[0])
        for m in list(range(n_dom - 1, 0, -1)):
            pay_copies[c, m].wait_recv()
            total[...] += dot_nt(terms(pay_recv[c, m], 2), drop[m])
        out_ref[pl.ds(c * size, size)] = fold(total[...], 2) * inverse
    for copy in core_copies + x_copies + list(meta_copies.values()) + list(pay_copies.values()):
        copy.wait_send()


def fused(leaf_hist, leaf_weight, leaf_parent, entry_parent, entry_dest, entry_crash, entry_weight):
    n_dom = lax.axis_size("dom")
    capacity = 4 * ENT_DEV // n_dom
    leaves = leaf_hist.shape[1]
    size = ROWS // CHUNKS
    vmem = pl.BlockSpec(memory_space=pltpu.VMEM)
    dma = pltpu.SemaphoreType.DMA
    row = lambda array: array.reshape(1, -1)
    return pl.pallas_call(
        functools.partial(fused_kernel, n_dom, capacity),
        out_shape=pltpu.VMEM((ROWS, CRASH_DEV), F32),
        in_specs=[pl.BlockSpec(memory_space=pltpu.HBM)] * 7,
        out_specs=vmem,
        scratch_shapes=[
            pltpu.VMEM((HIST * THICK, leaves), F32),
            pltpu.VMEM((1, leaves), F32),
            pltpu.VMEM((1, leaves), I32),
            pltpu.VMEM((1, ENT_DEV), I32),
            pltpu.VMEM((1, ENT_DEV), I32),
            pltpu.VMEM((1, ENT_DEV), I32),
            pltpu.VMEM((1, ENT_DEV), F32),
            pltpu.VMEM((2 * (HEAD + ROWS), leaves), BF16),
            pltpu.VMEM((2, HEAD + ROWS, PAR_DEV), F32),
            pltpu.VMEM((2, HEAD + ROWS, PAR_DEV), F32),
            pltpu.VMEM((2, HEAD + ROWS, PAR_DEV), F32),
            pltpu.VMEM((HEAD + ROWS, PAR_DEV), F32),
            pltpu.VMEM((HEAD + ROWS, PAR_DEV), F32),
            pltpu.VMEM((n_dom, 8, capacity), F32),
            pltpu.VMEM((n_dom, 8, capacity), F32),
            pltpu.VMEM((n_dom, PAR_DEV, capacity), BF16),
            pltpu.VMEM((n_dom, CRASH_DEV, capacity), BF16),
            pltpu.VMEM((CHUNKS, n_dom, size, capacity), F32),
            pltpu.VMEM((CHUNKS, n_dom, size, capacity), F32),
            pltpu.VMEM((2 * size, CRASH_DEV), F32),
            dma((7,)),
            dma((2,)),
            dma((2,)),
            dma((CHUNKS,)),
            dma((CHUNKS,)),
            dma((n_dom,)),
            dma((n_dom,)),
            dma((CHUNKS, n_dom)),
            dma((CHUNKS, n_dom)),
        ],
        compiler_params=pltpu.CompilerParams(
            collective_id=0, has_side_effects=True, vmem_limit_bytes=60 * 1024 * 1024
        ),
    )(
        leaf_hist, row(leaf_weight), row(leaf_parent), row(entry_parent), row(entry_dest), row(entry_crash),
        row(entry_weight),
    )


def solution(mesh):
    n_dom, n_sub = mesh.shape["dom"], mesh.shape["sub"]
    aligned = n_dom & (n_dom - 1) == 0 and n_dom <= 8 and (4 * ENT_DEV // n_dom) % 128 == 0 and n_sub == 4
    in_specs = (
        P(None, ("dom", "sub")),
        P(("dom", "sub")),
        P(("dom", "sub")),
        P(("dom", "sub")),
        P(("dom", "sub"), None),
        P(("dom", "sub")),
        P(("dom", "sub")),
    )
    out_specs = P(None, ("dom", "sub"))
    return jax.shard_map(
        fused if aligned else per_device, mesh=mesh, in_specs=in_specs, out_specs=out_specs, check_vma=False
    )
```

```python
import functools

import jax
import jax.numpy as jnp
from jax import lax
from jax.experimental import pallas as pl
from jax.experimental.pallas import tpu as pltpu
from jax.sharding import PartitionSpec as P

HIST = 16
THICK = 7
CTHICK = 5
PAR_DEV = 512
ENT_DEV = 512
CRASH_DEV = 512


def remap_table():
    target = jnp.arange(CTHICK, dtype=jnp.float32) * ((THICK - 1) / (CTHICK - 1))
    source = jnp.arange(THICK, dtype=jnp.float32)
    return jnp.maximum(0.0, 1.0 - jnp.abs(target[:, None] - source[None, :]))


def remap_rows(values):
    columns = values.shape[1]
    cube = values.reshape(HIST, THICK, columns)
    result = jnp.einsum("ct,htn->hcn", remap_table(), cube, precision=lax.Precision.HIGHEST)
    return result.reshape(HIST * CTHICK, columns)


def per_device(
    leaf_hist, leaf_weight, leaf_parent, entry_parent, entry_dest, entry_crash, entry_weight
):
    sub_total = lax.axis_size("sub")
    dom_total = lax.axis_size("dom")
    group_parents = PAR_DEV * sub_total
    weighted = (leaf_hist * leaf_weight[None, :]).T
    partial_sums = jax.ops.segment_sum(weighted, leaf_parent, num_segments=group_parents).T
    partial_weight = jax.ops.segment_sum(leaf_weight, leaf_parent, num_segments=group_parents)
    parent_sums, parent_weight = (
        lax.psum_scatter(partial_sums, "sub", scatter_dimension=1, tiled=True),
        lax.psum_scatter(partial_weight, "sub", scatter_dimension=0, tiled=True),
    )
    parent_hist = parent_sums / parent_weight[None, :]
    parent_hist = remap_rows(parent_hist)
    capacity = max(2, 4 * ENT_DEV // dom_total)
    slot_total = dom_total * capacity
    destination = entry_dest[:, 0]
    entry_total = destination.shape[0]
    ordering = jnp.argsort(destination, stable=True)
    sorted_destination = destination[ordering]
    first_slot = jnp.searchsorted(sorted_destination, sorted_destination, side="left")
    positions = jnp.arange(entry_total, dtype=jnp.int32)
    slot_sorted = sorted_destination * capacity + (positions - first_slot)
    slot_index = jnp.zeros((entry_total,), jnp.int32).at[ordering].set(slot_sorted)
    carried = jnp.take(parent_hist, entry_parent, axis=1) * entry_weight[None, :]
    send_values = (
        jnp.zeros((carried.shape[0], slot_total), jnp.float32).at[:, slot_index].set(carried)
    )
    send_weight = jnp.zeros((1, slot_total), jnp.float32).at[0, slot_index].set(entry_weight)
    send_crash = jnp.zeros((1, slot_total), jnp.int32).at[0, slot_index].set(entry_crash)
    got_values, got_weight, got_crash = (
        lax.all_to_all(send_values, "dom", split_axis=1, concat_axis=1, tiled=True),
        lax.all_to_all(send_weight, "dom", split_axis=1, concat_axis=1, tiled=True),
        lax.all_to_all(send_crash, "dom", split_axis=1, concat_axis=1, tiled=True),
    )
    crash_sums = jax.ops.segment_sum(got_values.T, got_crash[0], num_segments=CRASH_DEV).T
    crash_weight = jax.ops.segment_sum(got_weight[0], got_crash[0], num_segments=CRASH_DEV)
    return crash_sums / jnp.maximum(crash_weight, 1.0)[None, :]


MESH = pl.DeviceIdType.MESH
F32, BF16, I32 = jnp.float32, jnp.bfloat16, jnp.int32
HEAD = 8
ROWS = HIST * CTHICK
SIZES = (16, 64)
CHUNKS = len(SIZES)


def dot_nn(a, b):
    return lax.dot_general(a, b, (((1,), (0,)), ((), ())), preferred_element_type=F32)


def dot_nt(a, b):
    return lax.dot_general(a, b, (((1,), (1,)), ((), ())), preferred_element_type=F32)


def terms(x, count):
    parts = []
    for _ in range(count):
        part = x.astype(BF16).astype(F32)
        parts.append(part)
        x = x - part
    return jnp.concatenate(parts, axis=0).astype(BF16)


def fold(x, count):
    rows = x.shape[0] // count
    total = x[:rows]
    for i in range(1, count):
        total = total + x[i * rows : (i + 1) * rows]
    return total


def one_hot(index_row, rows):
    step = min(rows, 256)
    count = index_row.shape[1]
    iota = lax.broadcasted_iota(I32, (step, count), 0).astype(F32).astype(BF16)
    one, zero = jnp.ones((), BF16), jnp.zeros((), BF16)
    blocks = []
    for base in range(0, rows, step):
        low = index_row - base
        low = jnp.where((low >= 0) & (low < step), low, -1).astype(F32).astype(BF16)
        blocks.append(jnp.where(iota == low, one, zero))
    return jnp.concatenate(blocks, axis=0) if len(blocks) > 1 else blocks[0]


def remap_matrix():
    row = lax.broadcasted_iota(I32, (ROWS, HIST * THICK), 0)
    column = lax.broadcasted_iota(I32, (ROWS, HIST * THICK), 1)
    row_h = (row * 205) >> 10
    column_h = (column * 147) >> 10
    target = (row - row_h * CTHICK).astype(F32) * ((THICK - 1) / (CTHICK - 1))
    source = (column - column_h * THICK).astype(F32)
    weight = jnp.maximum(0.0, 1.0 - jnp.abs(target - source))
    return jnp.where(row_h == column_h, weight, 0.0).astype(BF16)


def fused_kernel(
    n_dom, capacity,
    hist_hbm, leaf_weight_hbm, leaf_parent_hbm, entry_parent_hbm, entry_dest_hbm, entry_crash_hbm, entry_weight_hbm,
    out_ref,
    hist, leaf_weight, leaf_parent, entry_parent, entry_dest, entry_crash, entry_weight, data, kept, core_send, core_recv, x_send, x_recv, meta, meta_recv, pick, drop, pay, pay_recv,
    load_sem, core_ssem, core_rsem, x_ssem, x_rsem, meta_ssem, meta_rsem, pay_ssem, pay_rsem,
):
    dom, sub = lax.axis_index("dom"), lax.axis_index("sub")
    pairs = [
        (leaf_parent_hbm, leaf_parent),
        (hist_hbm, hist),
        (leaf_weight_hbm, leaf_weight),
        (entry_dest_hbm, entry_dest),
        (entry_weight_hbm, entry_weight),
        (entry_crash_hbm, entry_crash),
        (entry_parent_hbm, entry_parent),
    ]
    loads = [pltpu.make_async_copy(source, target, load_sem.at[i]) for i, (source, target) in enumerate(pairs)]
    for load in loads:
        load.start()
    core = lax.rem(sub, 2)
    x = sub // 2
    core_peer = (dom, x * 2 + 1 - core)
    x_peer = (dom, (1 - x) * 2 + core)

    def dom_of(mask):
        peer = jnp.zeros((), I32)
        bit = 1
        while bit < n_dom:
            own = lax.rem(dom // bit, 2)
            peer = peer + bit * (1 - own if mask & bit else own)
            bit *= 2
        return peer

    dom_peers = [(dom_of(mask), sub) for mask in range(n_dom)]
    barrier = pltpu.get_barrier_semaphore()
    for peer in [core_peer, x_peer] + dom_peers[1:]:
        pl.semaphore_signal(barrier, inc=1, device_id=peer, device_id_type=MESH)

    def remote(source, target, ssem, rsem, peer):
        return pltpu.make_async_remote_copy(
            src_ref=source, dst_ref=target, send_sem=ssem, recv_sem=rsem, device_id=peer, device_id_type=MESH
        )

    loads[0].wait()
    first_hot = one_hot(leaf_parent[...] - ((1 - x) * 2 + 1 - core) * PAR_DEV, PAR_DEV)
    loads[1].wait()
    loads[2].wait()
    high = hist[...].astype(BF16)
    low = (hist[...] - high.astype(F32)).astype(BF16)
    table = remap_matrix()
    remapped = dot_nn(table, high) + dot_nn(table, low)
    weight = leaf_weight[...]
    first = lax.broadcasted_iota(I32, (HEAD, weight.shape[1]), 0) == 0
    head = jnp.where(first, weight, 0.0)
    data[...] = terms(jnp.concatenate([head, remapped * weight], axis=0), 2)

    def quarter(index):
        return fold(dot_nt(data[...], one_hot(leaf_parent[...] - index * PAR_DEV, PAR_DEV)), 2)

    core_copies = [
        remote(core_send.at[i], core_recv.at[i], core_ssem.at[i], core_rsem.at[i], core_peer) for i in range(2)
    ]
    bounds = [0] + [HEAD + sum(SIZES[: c + 1]) for c in range(CHUNKS)]
    places = [pl.ds(sum(SIZES[:c]), SIZES[c]) for c in range(CHUNKS)]
    spans = [pl.ds(bounds[c], bounds[c + 1] - bounds[c]) for c in range(CHUNKS)]
    x_copies = [
        remote(x_send.at[span], x_recv.at[span], x_ssem.at[c], x_rsem.at[c], x_peer) for c, span in enumerate(spans)
    ]
    core_send[0] = fold(dot_nt(data[...], first_hot), 2)
    pl.semaphore_wait(barrier, n_dom + 1)
    core_copies[0].start()
    kept[0] = quarter((1 - x) * 2 + core)
    core_copies[0].wait_recv()
    for c, span in enumerate(spans):
        x_send[span] = kept[0, span] + core_recv[0, span]
        x_copies[c].start()
    core_send[1] = quarter(x * 2 + 1 - core)
    core_copies[1].start()
    kept[1] = quarter(x * 2 + core)

    for load in loads[3:]:
        load.wait()
    entries = entry_parent.shape[1]
    named = entry_dest[...]
    mask = jnp.zeros_like(named)
    bit = 1
    while bit < n_dom:
        own = lax.rem(dom // bit, 2)
        part = lax.rem(named // bit, 2)
        mask = mask + bit * jnp.abs(part - own)
        bit *= 2
    padded = max(n_dom, 8)
    is_dest = (lax.broadcasted_iota(I32, (padded, entries), 0) == mask).astype(F32)
    earlier = lax.broadcasted_iota(I32, (entries, entries), 0) < lax.broadcasted_iota(I32, (entries, entries), 1)
    before = dot_nn(is_dest.astype(BF16), earlier.astype(F32).astype(BF16))
    rank = jnp.sum(before * is_dest, axis=0, keepdims=True).astype(I32)
    slot = mask * capacity + rank
    rows = jnp.concatenate(
        [
            entry_weight[...],
            entry_crash[...].astype(F32),
            entry_parent[...].astype(F32),
            jnp.zeros((5, entries), F32),
        ],
        axis=0,
    )
    rows = terms(rows, 3)
    for m in range(n_dom):
        meta[m] = fold(dot_nt(rows, one_hot(slot - m * capacity, capacity)), 3)
    meta_copies = {
        m: remote(meta.at[m], meta_recv.at[m], meta_ssem.at[m], meta_rsem.at[m], dom_peers[m])
        for m in range(1, n_dom)
    }
    for copy in meta_copies.values():
        copy.start()
    for m in range(n_dom):
        pick[m] = one_hot(meta[m, 2:3].astype(I32), PAR_DEV)

    core_copies[1].wait_recv()
    pay_copies = {}
    inverse = None
    for c, span in enumerate(spans):
        x_copies[c].wait_recv()
        sums = kept[1, span] + core_recv[1, span] + x_recv[span]
        if c == 0:
            inverse = 1.0 / sums[:1]
            sums = sums[HEAD:]
        means = terms(sums * inverse, 2)
        for m in list(range(n_dom - 1, -1, -1)):
            pay[m, places[c]] = fold(dot_nn(means, pick[m]), 2) * meta[m, :1]
            if m:
                copy = remote(pay.at[m, places[c]], pay_recv.at[m, places[c]], pay_ssem.at[c, m], pay_rsem.at[c, m], dom_peers[m])
                copy.start()
                pay_copies[c, m] = copy

    crash_weight = jnp.zeros((1, CRASH_DEV), F32)
    for m in range(n_dom):
        if m:
            meta_copies[m].wait_recv()
        got = meta_recv[m] if m else meta[0]
        drop[m] = one_hot(got[1:2].astype(I32), CRASH_DEV)
        crash_weight = crash_weight + fold(dot_nt(terms(got, 3), drop[m]), 3)[:1]
    inverse = 1.0 / jnp.maximum(crash_weight, 1.0)
    for c in range(CHUNKS):
        total = dot_nt(terms(pay[0, places[c]], 2), drop[0])
        for m in list(range(1, n_dom // 2)) + list(range(n_dom - 1, n_dom // 2 - 1, -1)):
            pay_copies[c, m].wait_recv()
            total += dot_nt(terms(pay_recv[m, places[c]], 2), drop[m])
        out_ref[places[c]] = fold(total, 2) * inverse
    for copy in core_copies + x_copies + list(meta_copies.values()) + list(pay_copies.values()):
        copy.wait_send()


def fused(leaf_hist, leaf_weight, leaf_parent, entry_parent, entry_dest, entry_crash, entry_weight):
    n_dom = lax.axis_size("dom")
    capacity = 4 * ENT_DEV // n_dom
    leaves = leaf_hist.shape[1]
    vmem = pl.BlockSpec(memory_space=pltpu.VMEM)
    dma = pltpu.SemaphoreType.DMA
    row = lambda array: array.reshape(1, -1)
    return pl.pallas_call(
        functools.partial(fused_kernel, n_dom, capacity),
        out_shape=pltpu.VMEM((ROWS, CRASH_DEV), F32),
        in_specs=[pl.BlockSpec(memory_space=pltpu.HBM)] * 7,
        out_specs=vmem,
        scratch_shapes=[
            pltpu.VMEM((HIST * THICK, leaves), F32),
            pltpu.VMEM((1, leaves), F32),
            pltpu.VMEM((1, leaves), I32),
            pltpu.VMEM((1, ENT_DEV), I32),
            pltpu.VMEM((1, ENT_DEV), I32),
            pltpu.VMEM((1, ENT_DEV), I32),
            pltpu.VMEM((1, ENT_DEV), F32),
            pltpu.VMEM((2 * (HEAD + ROWS), leaves), BF16),
            pltpu.VMEM((2, HEAD + ROWS, PAR_DEV), F32),
            pltpu.VMEM((2, HEAD + ROWS, PAR_DEV), F32),
            pltpu.VMEM((2, HEAD + ROWS, PAR_DEV), F32),
            pltpu.VMEM((HEAD + ROWS, PAR_DEV), F32),
            pltpu.VMEM((HEAD + ROWS, PAR_DEV), F32),
            pltpu.VMEM((n_dom, 8, capacity), F32),
            pltpu.VMEM((n_dom, 8, capacity), F32),
            pltpu.VMEM((n_dom, PAR_DEV, capacity), BF16),
            pltpu.VMEM((n_dom, CRASH_DEV, capacity), BF16),
            pltpu.VMEM((n_dom, ROWS, capacity), F32),
            pltpu.VMEM((n_dom, ROWS, capacity), F32),
            dma((7,)),
            dma((2,)),
            dma((2,)),
            dma((CHUNKS,)),
            dma((CHUNKS,)),
            dma((n_dom,)),
            dma((n_dom,)),
            dma((CHUNKS, n_dom)),
            dma((CHUNKS, n_dom)),
        ],
        compiler_params=pltpu.CompilerParams(
            collective_id=0, has_side_effects=True, vmem_limit_bytes=60 * 1024 * 1024
        ),
    )(
        leaf_hist, row(leaf_weight), row(leaf_parent), row(entry_parent), row(entry_dest), row(entry_crash),
        row(entry_weight),
    )


def solution(mesh):
    n_dom, n_sub = mesh.shape["dom"], mesh.shape["sub"]
    aligned = n_dom & (n_dom - 1) == 0 and n_dom <= 8 and (4 * ENT_DEV // n_dom) % 128 == 0 and n_sub == 4
    in_specs = (
        P(None, ("dom", "sub")),
        P(("dom", "sub")),
        P(("dom", "sub")),
        P(("dom", "sub")),
        P(("dom", "sub"), None),
        P(("dom", "sub")),
        P(("dom", "sub")),
    )
    out_specs = P(None, ("dom", "sub"))
    return jax.shard_map(
        fused if aligned else per_device, mesh=mesh, in_specs=in_specs, out_specs=out_specs, check_vma=False
    )
```
